32 devices in a mesh: patch: 8 (over z, y), mp: 4 (over x, core).
Axes of the slice: x: 2, y: 2, z: 4, core: 2. Of those that a mesh axis runs over, the one named last changes fastest.
Arguments:
- features: bfloat16 [4096, 1024], P('patch'), may hold values from -16 to 16
- gain_attn: float32 [1024], replicated, may hold values from 0.1 to 1.9
- w_qkv: bfloat16 [3, 1024, 1024], P(None, None, 'mp'), as said below
- w_out: bfloat16 [1024, 1024], P('mp'), may hold values from -0.1875 to 0.1875
- gain_mlp: float32 [1024], replicated, may hold values from 0.1 to 1.9
- w_up: bfloat16 [1024, 2048], P(None, 'mp'), may hold values from -0.1875 to 0.1875
- w_down: bfloat16 [2048, 1024], P('mp'), may hold values from -0.125 to 0.125
- neighbours: int32 [32, 8], replicated, may hold values from 0 to 31, as said below
Outputs:
- layer_out: bfloat16 [4096, 1024], P('patch', 'mp')
The draws below stay inside these ranges and needn't reach their ends.
Inputs may be any that keep to these rules, and one draw needn't show every extreme that they name: `neighbours`: row p lists 8 different patches; the first is p itself. Patch q belongs to device q // 4 of the patch axis, and every listed patch belongs to a device whose index differs from that of p's device by at most 2 around the patch axis (the lining closes into a cycle). `w_qkv`: projection weights of mean zero.
All inputs are finite; a program needn't handle non-finite values.
Results may differ from the reference program's by a relative error of at most 0.012.
Values may be sent and summed in bfloat16 or wider, within the bound.
A program may use at most 64 MiB of HBM per device.

```python
import jax
import jax.numpy as jnp
from jax import lax

D = 1024
H = 16
HD = 64
FF = 2048
PN = 128
K_NB = 8
REACH = 2
P_DEV = 4
NP = 32
NODES = 4096
N_MP = 4


def draw_neighbours(key, part):
    device_count = NP // P_DEV
    span = (2 * REACH + 1) * P_DEV
    patch_ids = jnp.arange(NP, dtype=jnp.int32)
    owner_dev = patch_ids // P_DEV
    candidate = jnp.arange(span, dtype=jnp.int32)
    cand_dev = jnp.mod(owner_dev[:, None] + candidate[None, :] // P_DEV - REACH, device_count)
    cand_ids = cand_dev * P_DEV + candidate[None, :] % P_DEV
    ranking = jax.random.randint(key, (NP, span), 0, 1 << 20, dtype=jnp.int32) * span + candidate[None, :]
    ranking = jnp.where(cand_ids == patch_ids[:, None], -1, ranking)
    ordering = jnp.argsort(ranking, axis=1)
    chosen = jnp.take_along_axis(cand_ids, ordering[:, :K_NB], axis=1)
    return chosen.astype(jnp.int32)


def draw_w_qkv(key, part):
    normal_base = jax.random.normal(key, (3, D, H * HD), jnp.float32) * D ** (-0.5)
    return normal_base.astype(jnp.bfloat16)


def draw_features(key, part):
    column_pos = jnp.arange(D, dtype=jnp.float32) / (D - 1.0)
    rough = jax.random.uniform(jax.random.fold_in(key, 3), (D,), jnp.float32, minval=0.7, maxval=1.3)
    col_scale = jnp.exp(jnp.log(0.35) + column_pos * (jnp.log(2.5) - jnp.log(0.35))) * rough
    base = jnp.clip(jax.random.normal(key, (NODES, D), jnp.float32), -5.0, 5.0)
    values = base * col_scale[None, :]
    return jnp.clip(values, -16.0, 16.0).astype(jnp.bfloat16)


def shard_levels(key, dims, cuts, low, top_value):
    loudness = 1.0
    for dim, shards_of in cuts:
        heights = jax.random.uniform(jax.random.fold_in(jax.random.fold_in(key, 6), dim), (shards_of,), jnp.float32, low / len(cuts), top_value / len(cuts))
        loudness = loudness * jnp.repeat(jnp.exp(heights), dims[dim] // shards_of).reshape((-1,) + (1,) * (len(dims) - 1 - dim))
    return loudness


def noise(own_key, dims, scale, most, split=(), held_as=jnp.bfloat16):
    level = shard_levels(own_key, dims, split, -0.22, 0.18) if split else 1.0
    array = jax.random.normal(own_key, dims, jnp.float32) * scale * level
    return jnp.minimum(jnp.maximum(array, -most), most).astype(held_as)


def setup_inputs(seed: int = 0) -> dict:
    streams_of = jax.random.split(jax.random.key(seed), 9)
    features = draw_features(jax.random.fold_in(streams_of[8], 71), 0)
    gain_attn = jnp.clip(1.0 + 0.18 * jax.random.normal(streams_of[1], (D,), jnp.float32), 0.1, 1.9)
    w_qkv = draw_w_qkv(jax.random.fold_in(streams_of[8], 71), 0)
    w_out = noise(streams_of[3], (H * HD, D), (H * HD) ** -0.5, 0.1875, ((0, 4),))
    gain_mlp = jnp.clip(1.0 + 0.18 * jax.random.normal(streams_of[4], (D,), jnp.float32), 0.1, 1.9)
    w_up = noise(streams_of[5], (D, FF), D ** -0.5, 0.1875, ((1, 4),))
    w_down = noise(streams_of[6], (FF, D), FF ** -0.5, 0.125, ((0, 4),))
    neighbours = draw_neighbours(jax.random.fold_in(streams_of[8], 71), 0)
    return dict(features=features, gain_attn=gain_attn, w_qkv=w_qkv, w_out=w_out, gain_mlp=gain_mlp, w_up=w_up, w_down=w_down, neighbours=neighbours)


def rms_norm(rows, gain):
    rows32 = rows.astype(jnp.float32)
    mean_sq = lax.optimization_barrier(jnp.mean(rows32 * rows32, axis=-1, keepdims=True))
    return (rows32 * lax.rsqrt(mean_sq + 1e-05) * gain).astype(jnp.bfloat16)

def group_sum(left, right, groups):
    width = left.shape[1] // groups
    total = jnp.zeros((left.shape[0], right.shape[1]), jnp.float32)
    for which in range(groups):
        term = jnp.dot(left[:, which * width:(which + 1) * width], right[which * width:(which + 1) * width], preferred_element_type=jnp.float32).astype(jnp.bfloat16)
        term = lax.optimization_barrier(term)
        total = total + term.astype(jnp.float32)
    return total

def reference(features, gain_attn, w_qkv, w_out, gain_mlp, w_up, w_down, neighbours):
    node_count = features.shape[0]
    normed = rms_norm(features, gain_attn)
    queries = jnp.dot(normed, w_qkv[0], preferred_element_type=jnp.float32).astype(jnp.bfloat16).reshape(NP, PN, H, HD)
    keys = jnp.dot(normed, w_qkv[1], preferred_element_type=jnp.float32).astype(jnp.bfloat16).reshape(NP, PN, H, HD)
    values = jnp.dot(normed, w_qkv[2], preferred_element_type=jnp.float32).astype(jnp.bfloat16).reshape(NP, PN, H, HD)
    scale_factor = 1.0 / HD ** 0.5

    def one_patch(inputs):
        query_blk, listed = inputs
        key_blk = keys[listed].reshape(K_NB * PN, H, HD)
        value_blk = values[listed].reshape(K_NB * PN, H, HD)
        scores = jnp.einsum('qhd,khd->hqk', query_blk.astype(jnp.float32), key_blk.astype(jnp.float32)) * scale_factor
        probs = jax.nn.softmax(scores, axis=-1).astype(jnp.bfloat16)
        mixed_rows = jnp.einsum('hqk,khd->qhd', probs.astype(jnp.float32), value_blk.astype(jnp.float32))
        return mixed_rows.astype(jnp.bfloat16).reshape(PN, H * HD)
    attended = lax.map(one_patch, (queries, neighbours)).reshape(node_count, H * HD)
    residual = features.astype(jnp.float32) + group_sum(attended, w_out, N_MP)
    normed2 = rms_norm(residual, gain_mlp)
    hidden = jax.nn.gelu(jnp.dot(normed2, w_up, preferred_element_type=jnp.float32), approximate=True).astype(jnp.bfloat16)
    return (residual + group_sum(hidden, w_down, N_MP)).astype(jnp.bfloat16)
```

```python
import functools

import jax
import jax.numpy as jnp
from jax import lax
from jax.experimental import pallas as pl
from jax.experimental.pallas import tpu as pltpu
from jax.sharding import PartitionSpec as P

HD = 64
PN = 128
K_NB = 8
REACH = 2
N_MP = 4
MESH = pl.DeviceIdType.MESH
F32 = jnp.float32
BF16 = jnp.bfloat16


def rms(rows, gain):
    mean_sq = jnp.mean(rows * rows, axis=-1, keepdims=True)
    return (rows * lax.rsqrt(mean_sq + 1e-05) * gain).astype(BF16)


def kernel(
    n, per, nb, feats, gain_attn, w_qkv, w_out_in, gain_mlp, w_up_in, w_down_in, out,
    win, normed, stacked, near, w_out, w_up, w_down, att, res, down, half, part, last,
    local_sem, halo_s, halo_r, w_s, w_r, att_s, att_r, rs1_s, rs1_r, rs2_s, rs2_r,
):
    p = lax.axis_index("patch")
    m = lax.axis_index("mp")
    odd = lax.rem(p, 2)
    twin = p + 1 - 2 * odd
    ahead = lax.rem(p + REACH, n)
    behind = lax.rem(p + n - REACH, n)
    lo = lax.rem(m, 2)
    hi = m // 2
    m1 = m + 1 - 2 * lo
    m2 = m + 2 - 4 * hi
    width = att.shape[-1]
    own = REACH * per

    local = [
        pltpu.make_async_copy(w_out_in, w_out.at[m], local_sem.at[0]),
        pltpu.make_async_copy(w_up_in, w_up, local_sem.at[1]),
        pltpu.make_async_copy(w_down_in, w_down, local_sem.at[2]),
    ]
    for copy in local:
        copy.start()

    barrier = pltpu.get_barrier_semaphore()
    for peer in (ahead, behind, twin):
        pl.semaphore_signal(barrier, inc=1, device_id={"patch": peer}, device_id_type=MESH)
    for peer in (m1, m2):
        pl.semaphore_signal(barrier, inc=1, device_id={"mp": peer}, device_id_type=MESH)
    pl.semaphore_wait(barrier, 5)

    def remote(src, dst, send, recv, where):
        return pltpu.make_async_remote_copy(
            src_ref=src, dst_ref=dst, send_sem=send, recv_sem=recv, device_id=where, device_id_type=MESH
        )

    def halo(kind, c):
        if kind == 0:
            src, dst, where = own + c, c, ahead
        elif kind == 1:
            src, dst, where = own + c, 4 * per + c, behind
        elif kind == 2:
            src, dst, where = own + c, (1 + 2 * odd) * per + c, twin
        else:
            src, dst, where = (4 - 4 * odd) * per + c, (3 - 2 * odd) * per + c, twin
        return remote(win.at[src], win.at[dst], halo_s.at[kind, c], halo_r.at[kind, c], {"patch": where})

    def halo_arrived(kind, c):
        dst = win.at[own + c]
        remote(dst, dst, halo_s.at[3, c], halo_r.at[kind, c], {"patch": twin}).wait_recv()

    def weight(kind):
        block = w_out.at[m if kind < 2 else m2]
        return remote(block, block, w_s.at[kind], w_r.at[kind], {"mp": m2 if kind == 0 else m1})

    def gather(kind, c):
        block = att.at[c, m if kind < 2 else m2]
        return remote(block, block, att_s.at[kind, c], att_r.at[kind, c], {"mp": m2 if kind == 0 else m1})

    def first_sum(c):
        return remote(down.at[c, 1 - lo], half.at[c], rs1_s.at[c], rs1_r.at[c], {"mp": m1})

    def second_sum(c):
        return remote(part.at[c], last.at[c], rs2_s.at[c], rs2_r.at[c], {"mp": m2})

    def project(c, carry):
        rows = pl.ds(pl.multiple_of(c * PN, PN), PN)
        here = rms(feats[rows, :].astype(F32), gain_attn[...])
        normed[rows, :] = here
        win[own + c, :, :width] = jnp.dot(here, w_qkv[1], preferred_element_type=F32).astype(BF16)
        win[own + c, :, width:] = jnp.dot(here, w_qkv[2], preferred_element_type=F32).astype(BF16)
        for kind in (0, 1, 2):
            halo(kind, c).start()
        return carry

    lax.fori_loop(0, per, project, 0)

    local[0].wait()
    weight(0).start()
    weight(1).start()

    heads = width // HD
    head_of = lax.broadcasted_iota(jnp.int32, (PN, width), 1) // HD

    def query(c, carry):
        rows = pl.ds(pl.multiple_of(c * PN, PN), PN)
        q = jnp.dot(normed[rows, :], w_qkv[0], preferred_element_type=F32).astype(BF16).astype(F32) * (1.0 / HD**0.5)
        for h in range(heads):
            stacked[c, h * PN : (h + 1) * PN, :] = jnp.where(head_of == h, q, 0.0).astype(BF16)
        return carry

    lax.fori_loop(0, per, query, 0)

    def forward(c, carry):
        halo_arrived(1 - odd, c)
        halo(3, c).start()
        return carry

    lax.fori_loop(0, per, forward, 0)
    weight(0).wait_recv()
    weight(2).start()

    def arrived(c, carry):
        halo_arrived(odd, c)
        halo_arrived(2, c)
        halo_arrived(3, c)
        return carry

    lax.fori_loop(0, per, arrived, 0)

    def attend(c, carry):
        for j in range(K_NB):
            listed = nb[p * per + c, j]
            offset = lax.rem(listed // per - p + n + n // 2, n) - n // 2
            slot = jnp.clip((offset + REACH) * per + lax.rem(listed, per), 0, (2 * REACH + 1) * per - 1)
            near[j * PN : (j + 1) * PN, :] = win[slot]
        mixed = jnp.zeros((PN, width), F32)
        for h in range(0, heads, 2):
            scores = lax.dot_general(
                stacked[c, h * PN : (h + 2) * PN, :], near[:, :width], (((1,), (1,)), ((), ())),
                preferred_element_type=F32,
            )
            top = jnp.max(scores, axis=-1, keepdims=True)
            e = jnp.exp(scores - top)
            total = jnp.sum(e, axis=-1, keepdims=True)
            o = jnp.dot(e.astype(BF16), near[:, width:], preferred_element_type=F32) / total
            mixed = jnp.where(head_of == h, o[:PN], mixed)
            mixed = jnp.where(head_of == h + 1, o[PN:], mixed)
        att[c, m] = mixed.astype(BF16)
        gather(0, c).start()
        gather(1, c).start()

        @pl.when(c > 0)
        def _():
            gather(0, c - 1).wait_recv()
            gather(2, c - 1).start()

        return carry

    lax.fori_loop(0, per, attend, 0)
    weight(1).wait_recv()
    weight(2).wait_recv()
    local[1].wait()
    local[2].wait()

    def add_up(c):
        first_sum(c).wait_recv()
        part[c] = (down[c, lo, 1 - hi].astype(F32) + half[c, 1 - hi].astype(F32)).astype(BF16)
        second_sum(c).start()

    def mlp(c, carry):
        @pl.when(c == 0)
        def _():
            gather(0, per - 1).wait_recv()
            gather(2, per - 1).start()

        gather(1, c).wait_recv()
        gather(2, c).wait_recv()
        rows = pl.ds(pl.multiple_of(c * PN, PN), PN)
        residual = feats[rows, :].astype(F32)
        for g in range(N_MP):
            residual = residual + jnp.dot(att[c, g], w_out[g], preferred_element_type=F32)
        for g in range(N_MP):
            res[c, g] = residual[:, g * width : (g + 1) * width]
        normed2 = rms(residual, gain_mlp[...])
        hidden = jax.nn.gelu(jnp.dot(normed2, w_up[...], preferred_element_type=F32), approximate=True).astype(BF16)
        for g in range(N_MP):
            down[c, g % 2, g // 2] = jnp.dot(
                hidden, w_down[:, g * width : (g + 1) * width], preferred_element_type=F32
            ).astype(BF16)
        first_sum(c).start()

        @pl.when(c > 0)
        def _():
            add_up(c - 1)

        return carry

    lax.fori_loop(0, per, mlp, 0)
    add_up(per - 1)

    def finish(c, carry):
        second_sum(c).wait_recv()
        rows = pl.ds(pl.multiple_of(c * PN, PN), PN)
        total = down[c, lo, hi].astype(F32) + half[c, hi].astype(F32) + last[c].astype(F32)
        out[rows, :] = (res[c, m] + total).astype(BF16)
        return carry

    lax.fori_loop(0, per, finish, 0)

    def sent(c, carry):
        for kind in range(4):
            halo(kind, c).wait_send()
        for kind in range(3):
            gather(kind, c).wait_send()
        first_sum(c).wait_send()
        second_sum(c).wait_send()
        return carry

    lax.fori_loop(0, per, sent, 0)
    for kind in range(3):
        weight(kind).wait_send()


def per_device(n, features, gain_attn, w_qkv, w_out, gain_mlp, w_up, w_down, neighbours):
    rows, d = features.shape
    per = rows // PN
    width = w_qkv.shape[2]
    heads = width // HD
    units = w_up.shape[1]
    vmem = pl.BlockSpec(memory_space=pltpu.VMEM)
    anywhere = pl.BlockSpec(memory_space=pl.ANY)
    dma = pltpu.SemaphoreType.DMA
    return pl.pallas_call(
        functools.partial(kernel, n, per),
        out_shape=jax.ShapeDtypeStruct((rows, d // N_MP), BF16),
        in_specs=[
            pl.BlockSpec(memory_space=pltpu.SMEM), vmem, vmem, vmem, anywhere, vmem, anywhere, anywhere,
        ],
        out_specs=vmem,
        scratch_shapes=[
            pltpu.VMEM(((2 * REACH + 1) * per, PN, 2 * width), BF16),
            pltpu.VMEM((rows, d), BF16),
            pltpu.VMEM((per, heads * PN, width), BF16),
            pltpu.VMEM((K_NB * PN, 2 * width), BF16),
            pltpu.VMEM((N_MP, width, d), BF16),
            pltpu.VMEM((d, units), BF16),
            pltpu.VMEM((units, d), BF16),
            pltpu.VMEM((per, N_MP, PN, width), BF16),
            pltpu.VMEM((per, N_MP, PN, width), F32),
            pltpu.VMEM((per, 2, 2, PN, width), BF16),
            pltpu.VMEM((per, 2, PN, width), BF16),
            pltpu.VMEM((per, PN, width), BF16),
            pltpu.VMEM((per, PN, width), BF16),
            dma((3,)), dma((4, per)), dma((4, per)), dma((3,)), dma((3,)), dma((3, per)), dma((3, per)),
            dma((per,)), dma((per,)), dma((per,)), dma((per,)),
        ],
        compiler_params=pltpu.CompilerParams(
            collective_id=0, has_side_effects=True, vmem_limit_bytes=48 * 1024 * 1024
        ),
    )(neighbours, features, gain_attn.reshape(1, d), w_qkv, w_out, gain_mlp.reshape(1, d), w_up, w_down)


def solution(mesh):
    return jax.shard_map(
        functools.partial(per_device, mesh.shape["patch"]),
        mesh=mesh,
        in_specs=(
            P("patch", None),
            P(),
            P(None, None, "mp"),
            P("mp", None),
            P(),
            P(None, "mp"),
            P("mp", None),
            P(),
        ),
        out_specs=P("patch", "mp"),
        check_vma=False,
    )
```

```python
import functools

import jax
import jax.numpy as jnp
from jax import lax
from jax.experimental import pallas as pl
from jax.experimental.pallas import tpu as pltpu
from jax.sharding import PartitionSpec as P

HD = 64
PN = 128
K_NB = 8
REACH = 2
N_MP = 4
MESH = pl.DeviceIdType.MESH
F32 = jnp.float32
BF16 = jnp.bfloat16


def rms(rows, gain):
    mean_sq = jnp.mean(rows * rows, axis=-1, keepdims=True)
    return (rows * lax.rsqrt(mean_sq + 1e-05) * gain).astype(BF16)


def kernel(
    n, per, nb, feats_in, gain_attn_in, w_qkv_in, w_out_in, gain_mlp_in, w_up_in, w_down_in, out,
    feats, gains, w_qkv, win, normed, stacked, near, w_out, w_up, w_down, att, res, down, half, part, last,
    local_sem, halo_s, halo_r, w_s, w_r, att_s, att_r, rs1_s, rs1_r, rs2_s, rs2_r,
):
    p = lax.axis_index("patch")
    m = lax.axis_index("mp")
    odd = lax.rem(p, 2)
    twin = p + 1 - 2 * odd
    ahead = lax.rem(p + REACH, n)
    behind = lax.rem(p + n - REACH, n)
    lo = lax.rem(m, 2)
    hi = m // 2
    m1 = m + 1 - 2 * lo
    m2 = m + 2 - 4 * hi
    width = att.shape[-1]
    own = REACH * per

    def take(which):
        if which < per:
            rows = pl.ds(which * PN, PN)
            src, dst = feats_in.at[rows], feats.at[rows]
        elif which < per + 3:
            src, dst = w_qkv_in.at[which - per], w_qkv.at[which - per]
        else:
            src, dst = (
                (gain_attn_in, gains.at[0]), (w_out_in, w_out.at[m]), (gain_mlp_in, gains.at[1]),
                (w_up_in, w_up), (w_down_in, w_down),
            )[which - per - 3]
        return pltpu.make_async_copy(src, dst, local_sem.at[which])

    take_q, take_k, take_v = per, per + 1, per + 2
    take_gain, take_out, take_gain2, take_up, take_down = range(per + 3, per + 8)
    for which in (take_gain, 0, take_k, take_v, *range(1, per), take_out, take_q, take_gain2, take_up, take_down):
        take(which).start()

    barrier = pltpu.get_barrier_semaphore()
    for peer in (ahead, behind, twin):
        pl.semaphore_signal(barrier, inc=1, device_id={"patch": peer}, device_id_type=MESH)
    for peer in (m1, m2):
        pl.semaphore_signal(barrier, inc=1, device_id={"mp": peer}, device_id_type=MESH)
    pl.semaphore_wait(barrier, 5)

    def remote(src, dst, send, recv, where):
        return pltpu.make_async_remote_copy(
            src_ref=src, dst_ref=dst, send_sem=send, recv_sem=recv, device_id=where, device_id_type=MESH
        )

    def halo(kind, c):
        if kind == 0:
            src, dst, where = own + c, c, ahead
        elif kind == 1:
            src, dst, where = own + c, 4 * per + c, behind
        elif kind == 2:
            src, dst, where = own + c, (1 + 2 * odd) * per + c, twin
        else:
            src, dst, where = (4 - 4 * odd) * per + c, (3 - 2 * odd) * per + c, twin
        return remote(win.at[src], win.at[dst], halo_s.at[kind, c], halo_r.at[kind, c], {"patch": where})

    def halo_arrived(kind, c):
        dst = win.at[own + c]
        remote(dst, dst, halo_s.at[3, c], halo_r.at[kind, c], {"patch": twin}).wait_recv()

    def weight(kind):
        block = w_out.at[m if kind < 2 else m2]
        return remote(block, block, w_s.at[kind], w_r.at[kind], {"mp": m2 if kind == 0 else m1})

    def gather(kind, c):
        block = att.at[c, m if kind < 2 else m2]
        return remote(block, block, att_s.at[kind, c], att_r.at[kind, c], {"mp": m2 if kind == 0 else m1})

    def first_sum(c):
        return remote(down.at[c, 1 - lo], half.at[c], rs1_s.at[c], rs1_r.at[c], {"mp": m1})

    def second_sum(c):
        return remote(part.at[c], last.at[c], rs2_s.at[c], rs2_r.at[c], {"mp": m2})

    for c in range(per):
        take(c).wait()
        if c == 0:
            take(take_gain).wait()
        here = rms(feats[c * PN : (c + 1) * PN, :].astype(F32), gains[0])
        normed[c * PN : (c + 1) * PN, :] = here
        if c == 0:
            take(take_k).wait()
        win[own + c, :, :width] = jnp.dot(here, w_qkv[1], preferred_element_type=F32).astype(BF16)
        if c == 0:
            take(take_v).wait()
        win[own + c, :, width:] = jnp.dot(here, w_qkv[2], preferred_element_type=F32).astype(BF16)
        for kind in (0, 1, 2):
            halo(kind, c).start()

    take(take_out).wait()
    weight(0).start()
    weight(1).start()

    heads = width // HD
    head_of = lax.broadcasted_iota(jnp.int32, (PN, width), 1) // HD

    def query(c, carry):
        rows = pl.ds(pl.multiple_of(c * PN, PN), PN)
        q = jnp.dot(normed[rows, :], w_qkv[0], preferred_element_type=F32).astype(BF16).astype(F32) * (1.0 / HD**0.5)
        for h in range(heads):
            stacked[c, h * PN : (h + 1) * PN, :] = jnp.where(head_of == h, q, 0.0).astype(BF16)
        return carry

    take(take_q).wait()
    lax.fori_loop(0, per, query, 0)

    def forward(c, carry):
        halo_arrived(1 - odd, c)
        halo(3, c).start()
        return carry

    lax.fori_loop(0, per, forward, 0)
    weight(0).wait_recv()
    weight(2).start()

    def arrived(c, carry):
        halo_arrived(odd, c)
        halo_arrived(2, c)
        halo_arrived(3, c)
        return carry

    lax.fori_loop(0, per, arrived, 0)

    def attend(c, carry):
        for j in range(K_NB):
            listed = nb[j, p * per + c]
            offset = lax.rem(listed // per - p + n + n // 2, n) - n // 2
            slot = jnp.clip((offset + REACH) * per + lax.rem(listed, per), 0, (2 * REACH + 1) * per - 1)
            near[j * PN : (j + 1) * PN, :] = win[slot]
        mixed = jnp.zeros((PN, width), F32)
        for h in range(0, heads, 2):
            scores = lax.dot_general(
                stacked[c, h * PN : (h + 2) * PN, :], near[:, :width], (((1,), (1,)), ((), ())),
                preferred_element_type=F32,
            )
            top = jnp.max(scores, axis=-1, keepdims=True)
            e = jnp.exp(scores - top)
            total = jnp.sum(e, axis=-1, keepdims=True)
            o = jnp.dot(e.astype(BF16), near[:, width:], preferred_element_type=F32) / total
            mixed = jnp.where(head_of == h, o[:PN], mixed)
            mixed = jnp.where(head_of == h + 1, o[PN:], mixed)
        att[c, m] = mixed.astype(BF16)
        gather(0, c).start()
        gather(1, c).start()

        @pl.when(c > 0)
        def _():
            gather(0, c - 1).wait_recv()
            gather(2, c - 1).start()

        return carry

    lax.fori_loop(0, per, attend, 0)
    weight(1).wait_recv()
    weight(2).wait_recv()
    for which in (take_gain2, take_up, take_down):
        take(which).wait()

    def add_up(c):
        first_sum(c).wait_recv()
        part[c] = (down[c, lo, 1 - hi].astype(F32) + half[c, 1 - hi].astype(F32)).astype(BF16)
        second_sum(c).start()

    def mlp(c, carry):
        @pl.when(c == 0)
        def _():
            gather(0, per - 1).wait_recv()
            gather(2, per - 1).start()

        gather(1, c).wait_recv()
        gather(2, c).wait_recv()
        rows = pl.ds(pl.multiple_of(c * PN, PN), PN)
        residual = feats[rows, :].astype(F32)
        for g in range(N_MP):
            residual = residual + jnp.dot(att[c, g], w_out[g], preferred_element_type=F32)
        for g in range(N_MP):
            res[c, g] = residual[:, g * width : (g + 1) * width]
        normed2 = rms(residual, gains[1])
        hidden = jax.nn.gelu(jnp.dot(normed2, w_up[...], preferred_element_type=F32), approximate=True).astype(BF16)
        for g in range(N_MP):
            down[c, g % 2, g // 2] = jnp.dot(
                hidden, w_down[:, g * width : (g + 1) * width], preferred_element_type=F32
            ).astype(BF16)
        first_sum(c).start()

        @pl.when(c > 0)
        def _():
            add_up(c - 1)

        return carry

    lax.fori_loop(0, per, mlp, 0)
    add_up(per - 1)

    def finish(c, carry):
        second_sum(c).wait_recv()
        rows = pl.ds(pl.multiple_of(c * PN, PN), PN)
        total = down[c, lo, hi].astype(F32) + half[c, hi].astype(F32) + last[c].astype(F32)
        out[rows, :] = (res[c, m] + total).astype(BF16)
        return carry

    lax.fori_loop(0, per, finish, 0)

    def sent(c, carry):
        for kind in range(4):
            halo(kind, c).wait_send()
        for kind in range(3):
            gather(kind, c).wait_send()
        first_sum(c).wait_send()
        second_sum(c).wait_send()
        return carry

    lax.fori_loop(0, per, sent, 0)
    for kind in range(3):
        weight(kind).wait_send()


def per_device(n, features, gain_attn, w_qkv, w_out, gain_mlp, w_up, w_down, neighbours):
    rows, d = features.shape
    per = rows // PN
    width = w_qkv.shape[2]
    heads = width // HD
    units = w_up.shape[1]
    vmem = pl.BlockSpec(memory_space=pltpu.VMEM)
    anywhere = pl.BlockSpec(memory_space=pl.ANY)
    dma = pltpu.SemaphoreType.DMA
    return pl.pallas_call(
        functools.partial(kernel, n, per),
        out_shape=jax.ShapeDtypeStruct((rows, d // N_MP), BF16),
        in_specs=[pl.BlockSpec(memory_space=pltpu.SMEM)] + [anywhere] * 7,
        out_specs=vmem,
        scratch_shapes=[
            pltpu.VMEM((rows, d), BF16),
            pltpu.VMEM((2, 1, d), F32),
            pltpu.VMEM((3, d, width), BF16),
            pltpu.VMEM(((2 * REACH + 1) * per, PN, 2 * width), BF16),
            pltpu.VMEM((rows, d), BF16),
            pltpu.VMEM((per, heads * PN, width), BF16),
            pltpu.VMEM((K_NB * PN, 2 * width), BF16),
            pltpu.VMEM((N_MP, width, d), BF16),
            pltpu.VMEM((d, units), BF16),
            pltpu.VMEM((units, d), BF16),
            pltpu.VMEM((per, N_MP, PN, width), BF16),
            pltpu.VMEM((per, N_MP, PN, width), F32),
            pltpu.VMEM((per, 2, 2, PN, width), BF16),
            pltpu.VMEM((per, 2, PN, width), BF16),
            pltpu.VMEM((per, PN, width), BF16),
            pltpu.VMEM((per, PN, width), BF16),
            dma((per + 8,)), dma((4, per)), dma((4, per)), dma((3,)), dma((3,)), dma((3, per)), dma((3, per)),
            dma((per,)), dma((per,)), dma((per,)), dma((per,)),
        ],
        compiler_params=pltpu.CompilerParams(
            collective_id=0, has_side_effects=True, vmem_limit_bytes=62 * 1024 * 1024
        ),
    )(neighbours.T, features, gain_attn.reshape(1, d), w_qkv, w_out, gain_mlp.reshape(1, d), w_up, w_down)


def solution(mesh):
    return jax.shard_map(
        functools.partial(per_device, mesh.shape["patch"]),
        mesh=mesh,
        in_specs=(
            P("patch", None),
            P(),
            P(None, None, "mp"),
            P("mp", None),
            P(),
            P(None, "mp"),
            P("mp", None),
            P(),
        ),
        out_specs=P("patch", "mp"),
        check_vma=False,
    )
```

```python
import functools

import jax
import jax.numpy as jnp
from jax import lax
from jax.experimental import pallas as pl
from jax.experimental.pallas import tpu as pltpu
from jax.sharding import PartitionSpec as P

HD = 64
PN = 128
K_NB = 8
REACH = 2
N_MP = 4
MESH = pl.DeviceIdType.MESH
F32 = jnp.float32
BF16 = jnp.bfloat16


def rms(rows, gain):
    mean_sq = jnp.mean(rows * rows, axis=-1, keepdims=True)
    return (rows * lax.rsqrt(mean_sq + 1e-05) * gain).astype(BF16)


def kernel(
    n, per, nb, feats_in, gain_attn_in, w_qkv_in, w_out_in, gain_mlp_in, w_up_in, w_down_in, out,
    feats, gains, w_qkv, win, normed, stacked, near, w_out, w_up, w_down, att, res, down, half, part, last,
    local_sem, halo_s, halo_r, w_s, w_r, att_s, att_r, rs1_s, rs1_r, rs2_s, rs2_r,
):
    p = lax.axis_index("patch")
    m = lax.axis_index("mp")
    odd = lax.rem(p, 2)
    twin = p + 1 - 2 * odd
    ahead = lax.rem(p + REACH, n)
    behind = lax.rem(p + n - REACH, n)
    lo = lax.rem(m, 2)
    hi = m // 2
    m1 = m + 1 - 2 * lo
    m2 = m + 2 - 4 * hi
    width = att.shape[-1]
    own = REACH * per

    def take(which):
        if which < per:
            rows = pl.ds(which * PN, PN)
            src, dst = feats_in.at[rows], feats.at[rows]
        elif which < per + 3:
            src, dst = w_qkv_in.at[which - per], w_qkv.at[which - per]
        else:
            src, dst = (
                (gain_attn_in, gains.at[0]), (w_out_in, w_out.at[m]), (gain_mlp_in, gains.at[1]),
                (w_up_in, w_up), (w_down_in, w_down),
            )[which - per - 3]
        return pltpu.make_async_copy(src, dst, local_sem.at[which])

    take_q, take_k, take_v = per, per + 1, per + 2
    take_gain, take_out, take_gain2, take_up, take_down = range(per + 3, per + 8)
    for which in (take_gain, 0, take_k, take_v, *range(1, per), take_out, take_q, take_gain2, take_up, take_down):
        take(which).start()

    barrier = pltpu.get_barrier_semaphore()
    for peer in (ahead, behind, twin):
        pl.semaphore_signal(barrier, inc=1, device_id={"patch": peer}, device_id_type=MESH)
    for peer in (m1, m2):
        pl.semaphore_signal(barrier, inc=1, device_id={"mp": peer}, device_id_type=MESH)
    pl.semaphore_wait(barrier, 5)

    def remote(src, dst, send, recv, where):
        return pltpu.make_async_remote_copy(
            src_ref=src, dst_ref=dst, send_sem=send, recv_sem=recv, device_id=where, device_id_type=MESH
        )

    relayed, direct = 1 - odd, odd

    def reach(kind, c):
        where = lax.rem(p + n + REACH - 2 * REACH * kind, n)
        return remote(
            win.at[own + c], win.at[4 * per * kind + c], halo_s.at[kind, c], halo_r.at[kind, c], {"patch": where}
        )

    def halo(kind, c):
        if kind == 2:
            src, dst = own + c, (1 + 2 * odd) * per + c
        else:
            src, dst = (4 - 4 * odd) * per + c, (3 - 2 * odd) * per + c
        return remote(win.at[src], win.at[dst], halo_s.at[kind, c], halo_r.at[kind, c], {"patch": twin})

    def halo_arrived(kind, c):
        dst = win.at[own + c]
        remote(dst, dst, halo_s.at[3, c], halo_r.at[kind, c], {"patch": twin}).wait_recv()

    def weight(kind):
        block = w_out.at[m if kind < 2 else m2]
        return remote(block, block, w_s.at[kind], w_r.at[kind], {"mp": m2 if kind == 0 else m1})

    def gather(kind, c):
        block = att.at[c, m if kind < 2 else m2]
        return remote(block, block, att_s.at[kind, c], att_r.at[kind, c], {"mp": m2 if kind == 0 else m1})

    def first_sum(c):
        return remote(down.at[c, 1 - lo], half.at[c], rs1_s.at[c], rs1_r.at[c], {"mp": m1})

    def second_sum(c):
        return remote(part.at[c], last.at[c], rs2_s.at[c], rs2_r.at[c], {"mp": m2})

    for c in range(per):
        take(c).wait()
        if c == 0:
            take(take_gain).wait()
        here = rms(feats[c * PN : (c + 1) * PN, :].astype(F32), gains[0])
        normed[c * PN : (c + 1) * PN, :] = here
        if c == 0:
            take(take_k).wait()
        win[own + c, :, :width] = jnp.dot(here, w_qkv[1], preferred_element_type=F32).astype(BF16)
        if c == 0:
            take(take_v).wait()
        win[own + c, :, width:] = jnp.dot(here, w_qkv[2], preferred_element_type=F32).astype(BF16)
        reach(relayed, c).start()
        halo(2, c).start()

    take(take_out).wait()
    weight(0).start()
    weight(1).start()

    heads = width // HD
    head_of = lax.broadcasted_iota(jnp.int32, (PN, width), 1) // HD

    def query(c, carry):
        rows = pl.ds(pl.multiple_of(c * PN, PN), PN)
        q = jnp.dot(normed[rows, :], w_qkv[0], preferred_element_type=F32).astype(BF16).astype(F32) * (1.0 / HD**0.5)
        for h in range(heads):
            stacked[c, h * PN : (h + 1) * PN, :] = jnp.where(head_of == h, q, 0.0).astype(BF16)
        return carry

    take(take_q).wait()
    lax.fori_loop(0, per, query, 0)

    for c in range(per):
        halo_arrived(relayed, c)
        halo(3, c).start()
        if c == max(per - 2, 0):
            for d in range(per):
                reach(direct, d).start()
    weight(0).wait_recv()
    weight(2).start()

    def arrived(c, carry):
        halo_arrived(direct, c)
        halo_arrived(2, c)
        halo_arrived(3, c)
        return carry

    lax.fori_loop(0, per, arrived, 0)

    def pass_on(c):
        gather(0, c).wait_recv()
        gather(2, c).start()

    def attend(c, carry):
        for j in range(K_NB):
            listed = nb[j, p * per + c]
            offset = lax.rem(listed // per - p + n + n // 2, n) - n // 2
            slot = jnp.clip((offset + REACH) * per + lax.rem(listed, per), 0, (2 * REACH + 1) * per - 1)
            near[j * PN : (j + 1) * PN, :] = win[slot]
        mixed = jnp.zeros((PN, width), F32)
        for h in range(0, heads, 2):
            scores = lax.dot_general(
                stacked[c, h * PN : (h + 2) * PN, :], near[:, :width], (((1,), (1,)), ((), ())),
                preferred_element_type=F32,
            )
            top = jnp.max(scores, axis=-1, keepdims=True)
            e = jnp.exp(scores - top)
            total = jnp.sum(e, axis=-1, keepdims=True)
            o = jnp.dot(e.astype(BF16), near[:, width:], preferred_element_type=F32) / total
            mixed = jnp.where(head_of == h, o[:PN], mixed)
            mixed = jnp.where(head_of == h + 1, o[PN:], mixed)
        att[c, m] = mixed.astype(BF16)
        gather(0, c).start()
        gather(1, c).start()

        @pl.when(c > 1)
        def _():
            pass_on(c - 2)

        return carry

    lax.fori_loop(0, per, attend, 0)
    weight(1).wait_recv()
    weight(2).wait_recv()
    for which in (take_gain2, take_up, take_down):
        take(which).wait()

    def add_up(c):
        first_sum(c).wait_recv()
        part[c] = (down[c, lo, 1 - hi].astype(F32) + half[c, 1 - hi].astype(F32)).astype(BF16)
        second_sum(c).start()

    def mlp(c, carry):
        @pl.when(c < 2)
        def _():
            pass_on(per - 2 + c)

        gather(1, c).wait_recv()
        gather(2, c).wait_recv()
        rows = pl.ds(pl.multiple_of(c * PN, PN), PN)
        residual = feats[rows, :].astype(F32)
        for g in range(N_MP):
            residual = residual + jnp.dot(att[c, g], w_out[g], preferred_element_type=F32)
        for g in range(N_MP):
            res[c, g] = residual[:, g * width : (g + 1) * width]
        normed2 = rms(residual, gains[1])
        hidden = jax.nn.gelu(jnp.dot(normed2, w_up[...], preferred_element_type=F32), approximate=True).astype(BF16)
        for g in range(N_MP):
            down[c, g % 2, g // 2] = jnp.dot(
                hidden, w_down[:, g * width : (g + 1) * width], preferred_element_type=F32
            ).astype(BF16)
        first_sum(c).start()

        @pl.when(c > 0)
        def _():
            add_up(c - 1)

        return carry

    lax.fori_loop(0, per, mlp, 0)
    add_up(per - 1)

    def finish(c, carry):
        second_sum(c).wait_recv()
        rows = pl.ds(pl.multiple_of(c * PN, PN), PN)
        total = down[c, lo, hi].astype(F32) + half[c, hi].astype(F32) + last[c].astype(F32)
        out[rows, :] = (res[c, m] + total).astype(BF16)
        return carry

    lax.fori_loop(0, per, finish, 0)

    def sent(c, carry):
        for kind in range(2):
            reach(kind, c).wait_send()
        for kind in (2, 3):
            halo(kind, c).wait_send()
        for kind in range(3):
            gather(kind, c).wait_send()
        first_sum(c).wait_send()
        second_sum(c).wait_send()
        return carry

    lax.fori_loop(0, per, sent, 0)
    for kind in range(3):
        weight(kind).wait_send()


def per_device(n, features, gain_attn, w_qkv, w_out, gain_mlp, w_up, w_down, neighbours):
    rows, d = features.shape
    per = rows // PN
    width = w_qkv.shape[2]
    heads = width // HD
    units = w_up.shape[1]
    vmem = pl.BlockSpec(memory_space=pltpu.VMEM)
    anywhere = pl.BlockSpec(memory_space=pl.ANY)
    dma = pltpu.SemaphoreType.DMA
    return pl.pallas_call(
        functools.partial(kernel, n, per),
        out_shape=jax.ShapeDtypeStruct((rows, d // N_MP), BF16),
        in_specs=[pl.BlockSpec(memory_space=pltpu.SMEM)] + [anywhere] * 7,
        out_specs=vmem,
        scratch_shapes=[
            pltpu.VMEM((rows, d), BF16),
            pltpu.VMEM((2, 1, d), F32),
            pltpu.VMEM((3, d, width), BF16),
            pltpu.VMEM(((2 * REACH + 1) * per, PN, 2 * width), BF16),
            pltpu.VMEM((rows, d), BF16),
            pltpu.VMEM((per, heads * PN, width), BF16),
            pltpu.VMEM((K_NB * PN, 2 * width), BF16),
            pltpu.VMEM((N_MP, width, d), BF16),
            pltpu.VMEM((d, units), BF16),
            pltpu.VMEM((units, d), BF16),
            pltpu.VMEM((per, N_MP, PN, width), BF16),
            pltpu.VMEM((per, N_MP, PN, width), F32),
            pltpu.VMEM((per, 2, 2, PN, width), BF16),
            pltpu.VMEM((per, 2, PN, width), BF16),
            pltpu.VMEM((per, PN, width), BF16),
            pltpu.VMEM((per, PN, width), BF16),
            dma((per + 8,)), dma((4, per)), dma((4, per)), dma((3,)), dma((3,)), dma((3, per)), dma((3, per)),
            dma((per,)), dma((per,)), dma((per,)), dma((per,)),
        ],
        compiler_params=pltpu.CompilerParams(
            collective_id=0, has_side_effects=True, vmem_limit_bytes=62 * 1024 * 1024
        ),
    )(neighbours.T, features, gain_attn.reshape(1, d), w_qkv, w_out, gain_mlp.reshape(1, d), w_up, w_down)


def solution(mesh):
    return jax.shard_map(
        functools.partial(per_device, mesh.shape["patch"]),
        mesh=mesh,
        in_specs=(
            P("patch", None),
            P(),
            P(None, None, "mp"),
            P("mp", None),
            P(),
            P(None, "mp"),
            P("mp", None),
            P(),
        ),
        out_specs=P("patch", "mp"),
        check_vma=False,
    )
```
